32 devices in a mesh: blk: 16 (over z, y, core), shell: 2 (over x).
Axes of the slice: x: 2, y: 2, z: 4, core: 2. Of those that a mesh axis runs over, the one named last changes fastest.
Arguments:
- images: bfloat16 [8192, 2, 8192], P('blk', None, 'shell'), may hold values from -30 to 30
- references: bfloat16 [1024, 2, 8192], P('blk', None, 'shell'), may hold values from -0.12 to 0.12
- defocus: float32 [8192], P('blk'), may hold values from 20 to 60
- frequency_squared: float32 [8192], P('shell'), may hold values from 0.05 to 1
- shell_index: int32 [8192], P('shell'), may hold values from 0 to 63, never falling along the last dimension, each value on 1 to 256 neighbouring positions
- noise_power: float32 [64], replicated, may hold values from 0.5 to 4
- live_count: int32 [16], P('blk'), may hold values from 1 to 512, 5120 in all
Outputs:
- weighted_images: float32 [1024, 2, 8192], P('blk', None, 'shell')
- weighted_envelope: float32 [1024, 8192], P('blk', 'shell')
- log_evidence: float32 [8192], P('blk')
The draws below stay inside these ranges and needn't reach their ends.
Inputs may be any that keep to these rules, and one draw needn't show every extreme that they name: `shell_index`: shell numbers never fall along the pixels; a shell holds 1 to 256 pixels. `live_count`: the live particles of a block fill its first slots; some block is full.
All inputs are finite; a program needn't handle non-finite values.
Results may differ from the reference program's by a relative error of at most 0.0059.
Values may be sent and summed in bfloat16 or wider, within the bound.
A program may use at most 128 MiB of HBM per device.

```python
import math
import jax
import jax.numpy as jnp
import numpy as np
from jax import lax

PIX = 8192
SHELLS = 64
REF_DEV = 64
CAP = 512
STEPS = 2
BLOCKS = 16
REFS = 1024
PARTICLES = 8192
N_BLK = 16


def shared_fields(key):
    keys = jax.random.split(key, 3)
    references = 0.02 * jnp.clip(jax.random.normal(keys[0], (REFS, 2, PIX), jnp.float32), -6.0, 6.0)
    defocus = jax.random.uniform(keys[1], (PARTICLES,), jnp.float32, 20.0, 60.0)
    frequency = jax.random.uniform(keys[2], (PIX,), jnp.float32, 0.05, 1.0)
    return (references, defocus, frequency)


def draw_images(key, part):
    key = jax.random.fold_in(key, 3)
    images = jnp.clip(jax.random.normal(key, (PARTICLES, 2, PIX), jnp.float32), -6.0, 6.0)
    return images.astype(jnp.bfloat16)


def draw_references(key, part):
    references, defocus, frequency = shared_fields(key)
    return references.astype(jnp.bfloat16)


def draw_defocus(key, part):
    references, defocus, frequency = shared_fields(key)
    return defocus


def draw_frequency_squared(key, part):
    references, defocus, frequency = shared_fields(key)
    return frequency


def length_profile(count, total, limit, skew):
    loads = [(1 << 20) // math.isqrt(rank ** skew) + 1 for rank in range(2, count + 1)]
    rest, given = total - limit - (count - 1), [1] * (count - 1)
    while rest > 0:
        free = [i for i in range(count - 1) if given[i] < limit]
        whole, left = sum([loads[i] for i in free]), rest
        for i in free:
            extra = min(limit - given[i], max(1, left * loads[i] // whole), rest)
            given[i] = given[i] + extra
            rest = rest - extra
    return np.array([limit] + given)


def ragged(key, number_of, total, limit, slope):
    if number_of == 2:
        one = jax.random.randint(key, (), max(1, total - limit), min(limit, total - 1) + 1)
        return jnp.stack([one, total - one])
    tallies = jnp.asarray(length_profile(number_of, total, limit, slope), jnp.int32)
    couples = (number_of - 1) // 2
    source_of, sink = tallies[1:1 + 2 * couples:2], tallies[2:2 + 2 * couples:2]
    margin = jnp.minimum(source_of - 1, limit - sink)
    passed = jax.random.randint(jax.random.fold_in(key, 1), (couples,), 0, 1 << 20) % (margin + 1)
    tallies = tallies.at[1:1 + 2 * couples:2].set(source_of - passed).at[2:2 + 2 * couples:2].set(sink + passed)
    return tallies[jax.random.permutation(jax.random.fold_in(key, 2), number_of)]


def setup_inputs(seed: int = 0) -> dict:
    key_of = jax.random.split(jax.random.key(seed), 8)
    return {
        "images": draw_images(jax.random.fold_in(key_of[7], 71), 0),
        "references": draw_references(jax.random.fold_in(key_of[7], 71), 0),
        "defocus": draw_defocus(jax.random.fold_in(key_of[7], 71), 0),
        "frequency_squared": draw_frequency_squared(jax.random.fold_in(key_of[7], 71), 0),
        "shell_index": jnp.searchsorted(jnp.cumsum(ragged(key_of[4], SHELLS, PIX, 2 * PIX // SHELLS, 1)), jnp.arange(PIX), side="right").astype(jnp.int32),
        "noise_power": jnp.clip(jnp.exp(jax.random.uniform(key_of[5], (SHELLS,), jnp.float32, math.log(0.5), math.log(4.0))), 0.5, 4.0),
        "live_count": ragged(key_of[6], BLOCKS, BLOCKS * CAP * 5 // 8, CAP, 2).astype(jnp.int32),
    }


def prepare(image_rows, defocus_rows, frequency_squared, weight):
    contrast = -jnp.sin(defocus_rows[:, None] * frequency_squared[None, :] + 0.1)
    filtered = (image_rows.astype(jnp.float32) * (contrast * weight)[:, None, :]).astype(jnp.bfloat16)
    envelope = (contrast * contrast * (0.5 * weight)).astype(jnp.bfloat16)
    return filtered, envelope


def reference(images, references, defocus, frequency_squared, shell_index, noise_power, live_count):
    weight = 1.0 / noise_power[shell_index]
    ref_blocks = references.reshape(N_BLK, REF_DEV, 2, PIX)

    def block_rows(block):
        start = (block * CAP).astype(jnp.int32)
        image_rows = lax.dynamic_slice_in_dim(images, start, CAP, 0)
        defocus_rows = lax.dynamic_slice_in_dim(defocus, start, CAP, 0)
        return prepare(image_rows, defocus_rows, frequency_squared, weight)

    def posterior_of(block):
        filtered, envelope = block_rows(block)
        met = jnp.concatenate([ref_blocks[((block - cycle_step) % N_BLK).astype(jnp.int32)] for cycle_step in range(STEPS + 1)], 0)
        met_wide = met.astype(jnp.float32)
        reference_power = (jnp.square(met_wide[:, 0]) + jnp.square(met_wide[:, 1])).astype(jnp.bfloat16)
        crossed = jnp.einsum('rkp,ikp->ri', met_wide, filtered.astype(jnp.float32))
        quadratic = jnp.einsum('rp,ip->ri', reference_power.astype(jnp.float32), envelope.astype(jnp.float32))
        scores = crossed - quadratic
        live_slots = jnp.arange(CAP, dtype=jnp.int32) < live_count[block]
        highest = jnp.max(scores, axis=0)
        summed = jnp.sum(jnp.exp(scores - highest[None, :]), axis=0)
        evidence = jnp.where(live_slots, highest + jnp.log(summed), jnp.float32(0.0))
        posterior = jnp.where(live_slots[None, :], jnp.exp(scores - evidence[None, :]), jnp.float32(0.0)).astype(jnp.bfloat16)
        return posterior, evidence

    posteriors, evidences = lax.map(posterior_of, jnp.arange(N_BLK, dtype=jnp.int32))

    def owner_sums(owner_block):
        numerator = jnp.zeros((REF_DEV, 2, PIX), jnp.float32)
        denominator = jnp.zeros((REF_DEV, PIX), jnp.float32)
        for cycle_step in range(STEPS + 1):
            source = ((owner_block + cycle_step) % N_BLK).astype(jnp.int32)
            filtered, envelope = block_rows(source)
            posterior = posteriors[source][cycle_step * REF_DEV:(cycle_step + 1) * REF_DEV].astype(jnp.float32)
            numerator = numerator + jnp.einsum('ri,ikp->rkp', posterior, filtered.astype(jnp.float32))
            denominator = denominator + jnp.einsum('ri,ip->rp', posterior, envelope.astype(jnp.float32))
        return numerator, denominator

    numerators, denominators = lax.map(owner_sums, jnp.arange(N_BLK, dtype=jnp.int32))
    return numerators.reshape(REFS, 2, PIX), denominators.reshape(REFS, PIX), evidences.reshape(PARTICLES)
```

```python
import math

import jax
import jax.numpy as jnp
from jax import lax
from jax.sharding import PartitionSpec as P

CHUNKS = 2
TURN = 2.0 * math.pi


def passed_along(value, axis, steps):
    count = lax.axis_size(axis)
    pairs = [(source, (source + steps) % count) for source in range(count)]
    return lax.ppermute(value, axis, pairs)


def minus_sine(defocus, turns):
    shifted = defocus[:, None] * turns[None, :] + (0.1 / TURN - 0.25)
    rest = shifted - jnp.round(shifted)
    y = 0.25 - jnp.abs(rest)
    square = y * y
    coefficients = [TURN ** k / math.factorial(k) * (1 if k % 4 == 3 else -1) for k in (1, 3, 5, 7, 9, 11)]
    value = jnp.full_like(square, coefficients[-1])
    for coefficient in coefficients[-2::-1]:
        value = value * square + coefficient
    return value * y


def body(images, references, defocus, frequency_squared, shell_index, noise_power, live_count):
    capacity = images.shape[0]
    per_block, _, pixels = references.shape
    shells = noise_power.shape[0]
    first = passed_along(references, "blk", 1)
    second = passed_along(first, "blk", 1)
    defocus_1 = passed_along(defocus, "blk", -1)
    defocus_2 = passed_along(defocus, "blk", -2)
    lookup = jnp.where(
        jnp.arange(shells, dtype=jnp.int32)[:, None] == shell_index[None, :],
        noise_power[:, None],
        0.0,
    )
    weight = 1.0 / jnp.sum(lookup, axis=0)
    half_weight = 0.5 * weight
    turns = frequency_squared * (1.0 / TURN)
    contrast = minus_sine(defocus, turns)
    filtered = (images.astype(jnp.float32) * (contrast * weight)[:, None, :]).astype(jnp.bfloat16)
    envelope = (contrast * contrast * half_weight).astype(jnp.bfloat16)
    filtered, envelope = lax.optimization_barrier((filtered, envelope))

    def envelope_of(values):
        other = minus_sine(values, turns)
        return (other * other * half_weight).astype(jnp.bfloat16)

    def partial(block):
        wide = block.astype(jnp.float32)
        power = (jnp.square(wide[:, 0]) + jnp.square(wide[:, 1])).astype(jnp.bfloat16)
        crossed = jnp.einsum("rkp,ikp->ri", block, filtered, preferred_element_type=jnp.float32)
        quadratic = jnp.einsum("rp,ip->ri", power, envelope, preferred_element_type=jnp.float32)
        return crossed - quadratic

    parts = []
    for block in (references, first, second):
        mine = partial(block)
        parts.append(mine + passed_along(mine, "shell", 1))
    scores = jnp.concatenate(parts, 0)
    live_slots = jnp.arange(capacity, dtype=jnp.int32) < live_count[0]
    highest = jnp.max(scores, axis=0)
    summed = jnp.sum(jnp.exp(scores - highest[None, :]), axis=0)
    evidence = jnp.where(live_slots, highest + jnp.log(summed), 0.0)
    posterior = jnp.where(live_slots[None, :], jnp.exp(scores - evidence[None, :]), 0.0).astype(
        jnp.bfloat16
    )
    here, back_1, back_2 = [posterior[s * per_block : (s + 1) * per_block] for s in range(3)]
    width = pixels // CHUNKS
    columns = [slice(c * width, (c + 1) * width) for c in range(CHUNKS)]

    def sums(rows, cut):
        return jnp.einsum(
            "ri,ikp->rkp", rows, filtered[:, :, cut], preferred_element_type=jnp.float32
        )

    returned_1 = passed_along(back_1, "blk", -1)
    returned_2 = passed_along(back_2, "blk", -2)
    farther = [passed_along(sums(back_2, cut).astype(jnp.bfloat16), "blk", -1) for cut in columns]
    nearer = [
        passed_along((sums(back_1, cut) + got.astype(jnp.float32)).astype(jnp.bfloat16), "blk", -1)
        for cut, got in zip(columns, farther)
    ]
    numerator = jnp.concatenate(
        [sums(here, cut) + got.astype(jnp.float32) for cut, got in zip(columns, nearer)], 2
    )
    denominator = sum(
        jnp.einsum("ri,ip->rp", rows, values, preferred_element_type=jnp.float32)
        for rows, values in (
            (here, envelope),
            (returned_1, envelope_of(defocus_1)),
            (returned_2, envelope_of(defocus_2)),
        )
    )
    return (numerator, denominator, evidence)


def solution(mesh):
    return jax.shard_map(
        body,
        mesh=mesh,
        in_specs=(
            P("blk", None, "shell"),
            P("blk", None, "shell"),
            P("blk"),
            P("shell"),
            P("shell"),
            P(),
            P("blk"),
        ),
        out_specs=(P("blk", None, "shell"), P("blk", "shell"), P("blk")),
        check_vma=False,
    )
```

```python
import math

import jax
import jax.numpy as jnp
from jax import lax
from jax.sharding import PartitionSpec as P

CHUNKS = 2
TURN = 2.0 * math.pi


def passed_along(value, axis, steps):
    count = lax.axis_size(axis)
    pairs = [(source, (source + steps) % count) for source in range(count)]
    return lax.ppermute(value, axis, pairs)


def minus_sine(defocus, turns):
    shifted = defocus[:, None] * turns[None, :] + (0.1 / TURN - 0.25)
    rest = shifted - jnp.round(shifted)
    y = 0.25 - jnp.abs(rest)
    square = y * y
    coefficients = [TURN ** k / math.factorial(k) * (1 if k % 4 == 3 else -1) for k in (1, 3, 5, 7, 9, 11)]
    value = jnp.full_like(square, coefficients[-1])
    for coefficient in coefficients[-2::-1]:
        value = value * square + coefficient
    return value * y


def body(images, references, defocus, frequency_squared, shell_index, noise_power, live_count):
    capacity = images.shape[0]
    per_block, _, pixels = references.shape
    shells = noise_power.shape[0]
    first = passed_along(references, "blk", 1)
    defocus_1 = passed_along(defocus, "blk", -1)
    defocus_2 = passed_along(defocus, "blk", -2)
    lookup = jnp.where(
        jnp.arange(shells, dtype=jnp.int32)[:, None] == shell_index[None, :],
        noise_power[:, None],
        0.0,
    )
    weight = 1.0 / jnp.sum(lookup, axis=0)
    half_weight = 0.5 * weight
    turns = frequency_squared * (1.0 / TURN)
    width = pixels // CHUNKS
    columns = [slice(c * width, (c + 1) * width) for c in range(CHUNKS)]

    def envelope_of(values):
        other = minus_sine(values, turns)
        return (other * other * half_weight).astype(jnp.bfloat16)

    contrast = minus_sine(defocus, turns)
    filtered = (images.astype(jnp.float32) * (contrast * weight)[:, None, :]).astype(jnp.bfloat16)
    envelope = (contrast * contrast * half_weight).astype(jnp.bfloat16)
    first, envelope, filtered = lax.optimization_barrier((first, envelope, filtered))
    second = [passed_along(first[:, :, cut], "blk", 1) for cut in columns]

    def partial(block, cut):
        wide = block.astype(jnp.float32)
        power = (jnp.square(wide[:, 0]) + jnp.square(wide[:, 1])).astype(jnp.bfloat16)
        crossed = jnp.einsum(
            "rkp,ikp->ri", block, filtered[:, :, cut], preferred_element_type=jnp.float32
        )
        quadratic = jnp.einsum(
            "rp,ip->ri", power, envelope[:, cut], preferred_element_type=jnp.float32
        )
        return crossed - quadratic

    parts = []
    for pieces in ([(references, slice(None))], [(first, slice(None))], list(zip(second, columns))):
        mine = sum(partial(block, cut) for block, cut in pieces)
        parts.append(mine + passed_along(mine, "shell", 1))
    scores = jnp.concatenate(parts, 0)
    live_slots = jnp.arange(capacity, dtype=jnp.int32) < live_count[0]
    highest = jnp.max(scores, axis=0)
    summed = jnp.sum(jnp.exp(scores - highest[None, :]), axis=0)
    evidence = jnp.where(live_slots, highest + jnp.log(summed), 0.0)
    posterior = jnp.where(live_slots[None, :], jnp.exp(scores - evidence[None, :]), 0.0).astype(
        jnp.bfloat16
    )
    here, back_1, back_2 = [posterior[s * per_block : (s + 1) * per_block] for s in range(3)]

    def sums(rows, cut):
        return jnp.einsum(
            "ri,ikp->rkp", rows, filtered[:, :, cut], preferred_element_type=jnp.float32
        )

    leaving = [sums(back_2, cut).astype(jnp.bfloat16) for cut in columns]
    farther = [passed_along(value, "blk", -1) for value in leaving]
    sent_1, sent_2, _ = lax.optimization_barrier((back_1, back_2, leaving[-1]))
    returned_1 = passed_along(sent_1, "blk", -1)
    returned_2 = passed_along(sent_2, "blk", -2)
    nearer = [
        passed_along((sums(back_1, cut) + got.astype(jnp.float32)).astype(jnp.bfloat16), "blk", -1)
        for cut, got in zip(columns, farther)
    ]
    numerator = jnp.concatenate(
        [sums(here, cut) + got.astype(jnp.float32) for cut, got in zip(columns, nearer)], 2
    )
    denominator = sum(
        jnp.einsum("ri,ip->rp", rows, values, preferred_element_type=jnp.float32)
        for rows, values in (
            (here, envelope),
            (returned_1, envelope_of(defocus_1)),
            (returned_2, envelope_of(defocus_2)),
        )
    )
    return (numerator, denominator, evidence)


def solution(mesh):
    return jax.shard_map(
        body,
        mesh=mesh,
        in_specs=(
            P("blk", None, "shell"),
            P("blk", None, "shell"),
            P("blk"),
            P("shell"),
            P("shell"),
            P(),
            P("blk"),
        ),
        out_specs=(P("blk", None, "shell"), P("blk", "shell"), P("blk")),
        check_vma=False,
    )
```

```python
import math

import jax
import jax.numpy as jnp
from jax import lax
from jax.sharding import PartitionSpec as P

CHUNKS = 2
TURN = 2.0 * math.pi


def passed_along(value, axis, steps):
    count = lax.axis_size(axis)
    pairs = [(source, (source + steps) % count) for source in range(count)]
    return lax.ppermute(value, axis, pairs)


def passed_by_even(value, axis, steps):
    count = lax.axis_size(axis)
    pairs = [(source, (source + steps) % count) for source in range(0, count, 2)]
    return lax.ppermute(value, axis, pairs)


def minus_sine(defocus, turns):
    shifted = defocus[:, None] * turns[None, :] + (0.1 / TURN - 0.25)
    rest = shifted - jnp.round(shifted)
    y = 0.25 - jnp.abs(rest)
    square = y * y
    coefficients = [TURN ** k / math.factorial(k) * (1 if k % 4 == 3 else -1) for k in (1, 3, 5, 7, 9, 11)]
    value = jnp.full_like(square, coefficients[-1])
    for coefficient in coefficients[-2::-1]:
        value = value * square + coefficient
    return value * y


def body(images, references, defocus, frequency_squared, shell_index, noise_power, live_count):
    capacity = images.shape[0]
    per_block, _, pixels = references.shape
    shells = noise_power.shape[0]
    width = pixels // CHUNKS
    columns = [slice(c * width, (c + 1) * width) for c in range(CHUNKS)]
    own = [references[:, :, cut] for cut in columns]
    first = [passed_along(block, "blk", 1) for block in own]
    direct = [passed_by_even(block, "blk", 2) for block in own]
    lookup = jnp.where(
        jnp.arange(shells, dtype=jnp.int32)[:, None] == shell_index[None, :],
        noise_power[:, None],
        0.0,
    )
    weight = 1.0 / jnp.sum(lookup, axis=0)
    half_weight = 0.5 * weight
    turns = frequency_squared * (1.0 / TURN)
    def envelope_of(values):
        other = minus_sine(values, turns)
        return (other * other * half_weight).astype(jnp.bfloat16)

    envelope = envelope_of(defocus)
    envelope, defocus_later, first[0], direct[0] = lax.optimization_barrier(
        (envelope, defocus, first[0], direct[0])
    )
    contrast = minus_sine(defocus_later, turns)
    filtered = (images.astype(jnp.float32) * (contrast * weight)[:, None, :]).astype(jnp.bfloat16)
    filtered = lax.optimization_barrier(filtered)

    def partial(block, cut):
        wide = block.astype(jnp.float32)
        power = (jnp.square(wide[:, 0]) + jnp.square(wide[:, 1])).astype(jnp.bfloat16)
        crossed = jnp.einsum(
            "rkp,ikp->ri", block, filtered[:, :, cut], preferred_element_type=jnp.float32
        )
        quadratic = jnp.einsum(
            "rp,ip->ri", power, envelope[:, cut], preferred_element_type=jnp.float32
        )
        return crossed - quadratic

    parts = []
    mine = partial(references, slice(None))
    mine, filtered, first[1], direct[1] = lax.optimization_barrier(
        (mine, filtered, first[1], direct[1])
    )
    paired = [passed_by_even(block, "blk", 1) for block in first]
    even = lax.rem(lax.axis_index("blk"), 2) == 0
    second = [jnp.where(even, one, other) for one, other in zip(direct, paired)]
    defocus_sent = lax.optimization_barrier((defocus, mine))[0]
    defocus_1 = passed_along(defocus_sent, "blk", -1)
    defocus_2 = passed_along(defocus_sent, "blk", -2)
    parts.append(mine + passed_along(mine, "shell", 1))
    for pieces in (first, second):
        mine = sum(partial(block, cut) for block, cut in zip(pieces, columns))
        parts.append(mine + passed_along(mine, "shell", 1))
    scores = jnp.concatenate(parts, 0)
    live_slots = jnp.arange(capacity, dtype=jnp.int32) < live_count[0]
    highest = jnp.max(scores, axis=0)
    summed = jnp.sum(jnp.exp(scores - highest[None, :]), axis=0)
    evidence = jnp.where(live_slots, highest + jnp.log(summed), 0.0)
    posterior = jnp.where(live_slots[None, :], jnp.exp(scores - evidence[None, :]), 0.0).astype(
        jnp.bfloat16
    )
    here, back_1, back_2 = [posterior[s * per_block : (s + 1) * per_block] for s in range(3)]

    def sums(rows, cut):
        return jnp.einsum(
            "ri,ikp->rkp", rows, filtered[:, :, cut], preferred_element_type=jnp.float32
        )

    returned_1 = passed_along(back_1, "blk", -1)
    returned_2 = passed_along(back_2, "blk", -2)
    farther = [passed_along(sums(back_2, cut).astype(jnp.bfloat16), "blk", -1) for cut in columns]
    nearer = [
        passed_along((sums(back_1, cut) + got.astype(jnp.float32)).astype(jnp.bfloat16), "blk", -1)
        for cut, got in zip(columns, farther)
    ]
    numerator = jnp.concatenate(
        [sums(here, cut) + got.astype(jnp.float32) for cut, got in zip(columns, nearer)], 2
    )
    denominator = sum(
        jnp.einsum("ri,ip->rp", rows, values, preferred_element_type=jnp.float32)
        for rows, values in (
            (here, envelope),
            (returned_1, envelope_of(defocus_1)),
            (returned_2, envelope_of(defocus_2)),
        )
    )
    return (numerator, denominator, evidence)


def solution(mesh):
    return jax.shard_map(
        body,
        mesh=mesh,
        in_specs=(
            P("blk", None, "shell"),
            P("blk", None, "shell"),
            P("blk"),
            P("shell"),
            P("shell"),
            P(),
            P("blk"),
        ),
        out_specs=(P("blk", None, "shell"), P("blk", "shell"), P("blk")),
        check_vma=False,
    )
```

```python
import math

import jax
import jax.numpy as jnp
from jax import lax
from jax.sharding import PartitionSpec as P

CHUNKS = 2
TURN = 2.0 * math.pi


def passed_along(value, axis, steps):
    count = lax.axis_size(axis)
    pairs = [(source, (source + steps) % count) for source in range(count)]
    return lax.ppermute(value, axis, pairs)


def passed_by_even(value, axis, steps):
    count = lax.axis_size(axis)
    pairs = [(source, (source + steps) % count) for source in range(0, count, 2)]
    return lax.ppermute(value, axis, pairs)


def minus_sine(defocus, turns):
    shifted = defocus[:, None] * turns[None, :] + (0.1 / TURN - 0.25)
    rest = shifted - jnp.round(shifted)
    y = 0.25 - jnp.abs(rest)
    square = y * y
    coefficients = [TURN ** k / math.factorial(k) * (1 if k % 4 == 3 else -1) for k in (1, 3, 5, 7, 9, 11)]
    value = jnp.full_like(square, coefficients[-1])
    for coefficient in coefficients[-2::-1]:
        value = value * square + coefficient
    return value * y


def body(images, references, defocus, frequency_squared, shell_index, noise_power, live_count):
    capacity = images.shape[0]
    per_block, _, pixels = references.shape
    shells = noise_power.shape[0]
    first = passed_along(references, "blk", 1)
    direct = passed_by_even(references, "blk", 2)
    lookup = jnp.where(
        jnp.arange(shells, dtype=jnp.int32)[:, None] == shell_index[None, :],
        noise_power[:, None],
        0.0,
    )
    weight = 1.0 / jnp.sum(lookup, axis=0)
    half_weight = 0.5 * weight
    turns = frequency_squared * (1.0 / TURN)
    contrast = minus_sine(defocus, turns)
    filtered = (images.astype(jnp.float32) * (contrast * weight)[:, None, :]).astype(jnp.bfloat16)
    envelope = (contrast * contrast * half_weight).astype(jnp.bfloat16)
    filtered, envelope = lax.optimization_barrier((filtered, envelope))

    def envelope_of(values):
        other = minus_sine(values, turns)
        return (other * other * half_weight).astype(jnp.bfloat16)

    def partial(block):
        wide = block.astype(jnp.float32)
        power = (jnp.square(wide[:, 0]) + jnp.square(wide[:, 1])).astype(jnp.bfloat16)
        crossed = jnp.einsum("rkp,ikp->ri", block, filtered, preferred_element_type=jnp.float32)
        quadratic = jnp.einsum("rp,ip->ri", power, envelope, preferred_element_type=jnp.float32)
        return crossed - quadratic

    mine = partial(references)
    mine, defocus_sent = lax.optimization_barrier((mine, defocus))
    defocus_1 = passed_along(defocus_sent, "blk", -1)
    defocus_2 = passed_along(defocus_sent, "blk", -2)
    mine, first, direct, defocus_1, defocus_2 = lax.optimization_barrier(
        (mine, first, direct, defocus_1, defocus_2)
    )
    paired = passed_by_even(first, "blk", 1)
    parts = [mine + passed_along(mine, "shell", 1)]
    even = lax.rem(lax.axis_index("blk"), 2) == 0
    second = jnp.where(even, direct, paired)
    for block in (first, second):
        mine = partial(block)
        parts.append(mine + passed_along(mine, "shell", 1))
    scores = jnp.concatenate(parts, 0)
    live_slots = jnp.arange(capacity, dtype=jnp.int32) < live_count[0]
    highest = jnp.max(scores, axis=0)
    summed = jnp.sum(jnp.exp(scores - highest[None, :]), axis=0)
    evidence = jnp.where(live_slots, highest + jnp.log(summed), 0.0)
    posterior = jnp.where(live_slots[None, :], jnp.exp(scores - evidence[None, :]), 0.0).astype(
        jnp.bfloat16
    )
    here, back_1, back_2 = [posterior[s * per_block : (s + 1) * per_block] for s in range(3)]
    width = pixels // CHUNKS
    columns = [slice(c * width, (c + 1) * width) for c in range(CHUNKS)]

    def sums(rows, cut):
        return jnp.einsum(
            "ri,ikp->rkp", rows, filtered[:, :, cut], preferred_element_type=jnp.float32
        )

    returned_1 = passed_along(back_1, "blk", -1)
    returned_2 = passed_along(back_2, "blk", -2)
    farther = [passed_along(sums(back_2, cut).astype(jnp.bfloat16), "blk", -1) for cut in columns]
    joined = [
        (sums(back_1, cut) + got.astype(jnp.float32)).astype(jnp.bfloat16)
        for cut, got in zip(columns, farther)
    ]
    nearer = [passed_along(value, "blk", -1) for value in joined]
    defocus_2, _ = lax.optimization_barrier((defocus_2, joined[-1]))
    numerator = jnp.concatenate(
        [sums(here, cut) + got.astype(jnp.float32) for cut, got in zip(columns, nearer)], 2
    )
    denominator = sum(
        jnp.einsum("ri,ip->rp", rows, values, preferred_element_type=jnp.float32)
        for rows, values in (
            (here, envelope),
            (returned_1, envelope_of(defocus_1)),
            (returned_2, envelope_of(defocus_2)),
        )
    )
    return (numerator, denominator, evidence)


def solution(mesh):
    return jax.shard_map(
        body,
        mesh=mesh,
        in_specs=(
            P("blk", None, "shell"),
            P("blk", None, "shell"),
            P("blk"),
            P("shell"),
            P("shell"),
            P(),
            P("blk"),
        ),
        out_specs=(P("blk", None, "shell"), P("blk", "shell"), P("blk")),
        check_vma=False,
    )
```

```python
import math

import jax
import jax.numpy as jnp
from jax import lax
from jax.sharding import PartitionSpec as P

CHUNKS = 2
TURN = 2.0 * math.pi


def passed_along(value, axis, steps):
    count = lax.axis_size(axis)
    pairs = [(source, (source + steps) % count) for source in range(count)]
    return lax.ppermute(value, axis, pairs)


def passed_by_even(value, axis, steps):
    count = lax.axis_size(axis)
    pairs = [(source, (source + steps) % count) for source in range(0, count, 2)]
    return lax.ppermute(value, axis, pairs)


def minus_sine(defocus, turns):
    shifted = defocus[:, None] * turns[None, :] + (0.1 / TURN - 0.25)
    rest = shifted - jnp.round(shifted)
    y = 0.25 - jnp.abs(rest)
    square = y * y
    coefficients = [-6.283185159611165, 41.341654929343306, -81.6009981926032, 76.54965682039136, -39.535813709565026]
    value = jnp.full_like(square, coefficients[-1])
    for coefficient in coefficients[-2::-1]:
        value = value * square + coefficient
    return value * y


def body(images, references, defocus, frequency_squared, shell_index, noise_power, live_count):
    capacity = images.shape[0]
    per_block, _, pixels = references.shape
    shells = noise_power.shape[0]
    first = passed_along(references, "blk", 1)
    direct = passed_by_even(references, "blk", 2)
    lookup = jnp.where(
        jnp.arange(shells, dtype=jnp.int32)[:, None] == shell_index[None, :],
        noise_power[:, None],
        0.0,
    )
    weight = 1.0 / jnp.sum(lookup, axis=0)
    half_weight = 0.5 * weight
    turns = frequency_squared * (1.0 / TURN)
    contrast = minus_sine(defocus, turns)
    filtered = (images.astype(jnp.float32) * (contrast * weight)[:, None, :]).astype(jnp.bfloat16)
    envelope = (contrast * contrast * half_weight).astype(jnp.bfloat16)
    filtered, envelope = lax.optimization_barrier((filtered, envelope))

    def envelope_of(values):
        other = minus_sine(values, turns)
        return (other * other * half_weight).astype(jnp.bfloat16)

    def partial(block):
        wide = block.astype(jnp.float32)
        power = (jnp.square(wide[:, 0]) + jnp.square(wide[:, 1])).astype(jnp.bfloat16)
        crossed = jnp.einsum("rkp,ikp->ri", block, filtered, preferred_element_type=jnp.float32)
        quadratic = jnp.einsum("rp,ip->ri", power, envelope, preferred_element_type=jnp.float32)
        return crossed - quadratic

    mine = partial(references)
    mine, first, direct = lax.optimization_barrier((mine, first, direct))
    paired = passed_by_even(first, "blk", 1)
    parts = [mine + passed_along(mine, "shell", 1)]
    even = lax.rem(lax.axis_index("blk"), 2) == 0
    second = jnp.where(even, direct, paired)
    for block in (first, second):
        mine = partial(block)
        parts.append(mine + passed_along(mine, "shell", 1))
    scores = jnp.concatenate(parts, 0)
    live_slots = jnp.arange(capacity, dtype=jnp.int32) < live_count[0]
    highest = jnp.max(scores, axis=0)
    summed = jnp.sum(jnp.exp(scores - highest[None, :]), axis=0)
    evidence = jnp.where(live_slots, highest + jnp.log(summed), 0.0)
    posterior = jnp.where(live_slots[None, :], jnp.exp(scores - evidence[None, :]), 0.0).astype(
        jnp.bfloat16
    )
    here, back_1, back_2 = [posterior[s * per_block : (s + 1) * per_block] for s in range(3)]
    width = pixels // CHUNKS
    columns = [slice(c * width, (c + 1) * width) for c in range(CHUNKS)]

    def sums(rows, cut):
        return jnp.einsum(
            "ri,ikp->rkp", rows, filtered[:, :, cut], preferred_element_type=jnp.float32
        )

    high = lax.reduce_precision(defocus, 8, 7)
    middle = lax.reduce_precision(defocus - high, 8, 7)
    low = defocus - high - middle
    rows = jnp.stack([high, middle, low] + [jnp.zeros_like(low)] * 13).astype(jnp.bfloat16)

    def returned(values, steps):
        got = passed_along(jnp.concatenate([values, rows], 0), "blk", -steps)
        terms = got[per_block : per_block + 3].astype(jnp.float32)
        return got[:per_block], terms[0] + terms[1] + terms[2]

    returned_1, defocus_1 = returned(back_1, 1)
    returned_2, defocus_2 = returned(back_2, 2)
    farther = [passed_along(sums(back_2, cut).astype(jnp.bfloat16), "blk", -1) for cut in columns]
    joined = [
        (sums(back_1, cut) + got.astype(jnp.float32)).astype(jnp.bfloat16)
        for cut, got in zip(columns, farther)
    ]
    nearer = [passed_along(value, "blk", -1) for value in joined]
    defocus_2, here_later, _ = lax.optimization_barrier((defocus_2, here, joined[-1]))
    numerator = jnp.concatenate(
        [sums(here, cut) + got.astype(jnp.float32) for cut, got in zip(columns, nearer)], 2
    )
    denominator = sum(
        jnp.einsum("ri,ip->rp", block, values, preferred_element_type=jnp.float32)
        for block, values in (
            (here_later, envelope),
            (returned_1, envelope_of(defocus_1)),
            (returned_2, envelope_of(defocus_2)),
        )
    )
    return (numerator, denominator, evidence)


def solution(mesh):
    return jax.shard_map(
        body,
        mesh=mesh,
        in_specs=(
            P("blk", None, "shell"),
            P("blk", None, "shell"),
            P("blk"),
            P("shell"),
            P("shell"),
            P(),
            P("blk"),
        ),
        out_specs=(P("blk", None, "shell"), P("blk", "shell"), P("blk")),
        check_vma=False,
    )
```
